512 devices in a mesh: tok: 64 (over y_hi, x, z), head: 8 (over y_lo, core).
Axes of the slice: x: 4, y: 8 (y_hi: 2, y_lo: 4; y = y_hi * 4 + y_lo), z: 8, core: 2. Of those that a mesh axis runs over, the one named last changes fastest.
Arguments:
- context: bfloat16 [8, 16384, 1024], P(None, 'tok'), may hold values from -6 to 6
- ctx_gain: float32 [1024], replicated, may hold values from 0.1 to 1.9
- queries: bfloat16 [64, 512], P('tok', 'head'), may hold values from -110 to 110
- key_weight: bfloat16 [1024, 512], P(None, 'head'), may hold values from -0.1875 to 0.1875
- value_weight: bfloat16 [1024, 512], P(None, 'head'), may hold values from -0.1875 to 0.1875
- out_weight: bfloat16 [512, 4096], P('head', 'tok'), may hold values from -0.25 to 0.25
Outputs:
- latent_out: bfloat16 [64, 8, 4096], P('head', None, 'tok')
The draws below stay inside these ranges and needn't reach their ends.
All inputs are finite; a program needn't handle non-finite values.
Results may differ from the reference program's by a relative error of at most 0.0059.
The reference program's roundings to bfloat16 on the way (of `normed`, `keys` and `attended`) count: a program that leaves them out, or rounds other values in their place, can miss the bound.
Values may be sent and summed in bfloat16 or wider, within the bound.
A program may use at most 64 MiB of HBM per device.

```python
import math
import jax
import jax.numpy as jnp
from jax import lax

D = 1024
HEADS = 8
HD = 64
LAT = 64
DL = 4096
VIDEOS = 8
VTOK_DEV = 256
VTOK = 16384
HH = 512
N_TOK = 64


def draw_queries(key, part):
    key = jax.random.fold_in(key, 7)
    first, second = jax.random.split(key)
    base = jnp.clip(jax.random.normal(first, (LAT, HH), jnp.float32), -4.0, 4.0)
    scales = jnp.exp(jax.random.uniform(second, (LAT, 1), jnp.float32, math.log(0.5), math.log(5.0)))
    return (base * scales).astype(jnp.bfloat16)


def shard_levels(key, dims, pieces, low, top_value):
    factor_of = 1.0
    for dim, parts in pieces:
        steps = jax.random.uniform(jax.random.fold_in(jax.random.fold_in(key, 6), dim), (parts,), jnp.float32, low / len(pieces), top_value / len(pieces))
        factor_of = factor_of * jnp.repeat(jnp.exp(steps), dims[dim] // parts).reshape((-1,) + (1,) * (len(dims) - 1 - dim))
    return factor_of


def centred(key, extent, deviation, limit, pieces=(), dtype=jnp.bfloat16):
    entries = deviation * jax.random.normal(key, extent, jnp.float32)
    if pieces:
        entries = entries * shard_levels(key, extent, pieces, -0.22, 0.18)
    return jnp.clip(entries, -limit, limit).astype(dtype)


def setup_inputs(seed: int = 0) -> dict:
    streams_of = jax.random.split(jax.random.key(seed), 7)
    return {
        "context": centred(streams_of[0], (VIDEOS, VTOK, D), 1.0, 6.0, ((1, 64),)),
        "ctx_gain": jnp.clip(1.0 + 0.18 * jax.random.normal(streams_of[1], (D,), jnp.float32), 0.1, 1.9),
        "queries": draw_queries(jax.random.fold_in(streams_of[6], 71), 0),
        "key_weight": centred(streams_of[3], (D, HH), D ** -0.5, 0.1875, ((1, 8),)),
        "value_weight": centred(streams_of[4], (D, HH), D ** -0.5, 0.1875, ((1, 8),)),
        "out_weight": centred(streams_of[5], (HH, DL), HH ** -0.5, 0.25, ((0, 8), (1, 64))),
    }


def block_partial(block, ctx_gain, queries, key_weight, value_weight):
    data = block.astype(jnp.float32)
    meansq = lax.optimization_barrier(jnp.mean(data * data, axis=-1, keepdims=True))
    normed = (data * lax.rsqrt(meansq + 1e-06) * ctx_gain).astype(jnp.bfloat16)
    keys = jnp.dot(normed, key_weight, preferred_element_type=jnp.float32).astype(jnp.bfloat16)
    values = jnp.dot(normed, value_weight, preferred_element_type=jnp.float32).astype(jnp.bfloat16)
    query_heads = queries.astype(jnp.float32).reshape(LAT, HEADS, HD)
    key_heads = keys.astype(jnp.float32).reshape(VTOK_DEV, HEADS, HD)
    value_heads = values.astype(jnp.float32).reshape(VTOK_DEV, HEADS, HD)
    scores = jnp.einsum('lhd,thd->hlt', query_heads, key_heads) * HD ** (-0.5)
    block_max = lax.optimization_barrier(jnp.max(scores, axis=-1))
    expo = jnp.exp(scores - block_max[:, :, None])
    block_sum = lax.optimization_barrier(jnp.sum(expo, axis=-1))
    weights = expo.astype(jnp.bfloat16).astype(jnp.float32)
    block_acc = jnp.einsum('hlt,thd->lhd', weights, value_heads)
    return (block_max.T, block_sum.T, block_acc)

def one_video(video, ctx_gain, queries, key_weight, value_weight):
    blocks = video.reshape(N_TOK, VTOK_DEV, D)
    maxima, sums, accs = lax.map(lambda b: block_partial(b, ctx_gain, queries, key_weight, value_weight), blocks)
    top = lax.optimization_barrier(jnp.max(maxima, axis=0))
    factor = jnp.exp(maxima - top[None])
    total = lax.optimization_barrier(jnp.sum(sums * factor, axis=0))
    accum = lax.optimization_barrier(jnp.sum(accs * factor[:, :, :, None], axis=0))
    return (accum / total[:, :, None]).reshape(LAT, HH).astype(jnp.bfloat16)

def reference(context, ctx_gain, queries, key_weight, value_weight, out_weight):
    attended = lax.map(lambda v: one_video(v, ctx_gain, queries, key_weight, value_weight), context)
    attended = jnp.transpose(attended, (1, 0, 2)).reshape(LAT * VIDEOS, HH)
    result = jnp.dot(attended, out_weight, preferred_element_type=jnp.float32)
    return result.reshape(LAT, VIDEOS, DL).astype(jnp.bfloat16)
```

```python
import functools

import jax
import jax.numpy as jnp
from jax import lax
from jax.experimental import pallas as pl
from jax.experimental.pallas import tpu as pltpu
from jax.sharding import PartitionSpec as P

MESH = pl.DeviceIdType.MESH
HD = 64
GROUP = 16
RING = (2, 4, 8)
HOPS = (4, 1, 1)
OPPOSITE = (1, 2, 4)


def distance(k):
    return sum(min(a, n - a) * w for a, n, w in zip(k, RING, HOPS))


def opposite(k):
    return tuple((o - a) % n for o, a, n in zip(OPPOSITE, k, RING))


def ordered_offsets():
    every = [(a, b, c) for a in range(2) for b in range(4) for c in range(8)]
    half = []
    for k in sorted(every, key=lambda k: (distance(k), k)):
        if len(half) < 32 and opposite(k) not in half:
            half.append(k)
    return half + [opposite(k) for k in reversed(half)]


OFFSETS = ordered_offsets()
N = len(OFFSETS)


def kernel(
    ctx, gain, query, key_t, value_t, out_w, out,
    xbuf, gbuf, qin, wt, w, normed, kv, qs, qr, ps, pr, att, ar, wr,
    in_sem, x_sem, q_send, q_recv, p_send, p_recv, a_send, a_recv, w_send, w_recv, w_own,
):
    tok, head = lax.axis_index("tok"), lax.axis_index("head")
    yh, x, z = tok // 32, (tok // 8) % 4, tok % 8
    ys = [((yh + a) % 2) * 32 for a in range(2)]
    xs = [((x + a) % 4) * 8 for a in range(4)]
    zs = [(z + a) % 8 for a in range(8)]

    def at(k):
        return ys[k[0]] + xs[k[1]] + zs[k[2]]

    videos = ctx.shape[0]
    small = [
        pltpu.make_async_copy(query, qin, in_sem.at[0]),
        pltpu.make_async_copy(value_t, wt.at[pl.ds(0, HD)], in_sem.at[1]),
        pltpu.make_async_copy(key_t, wt.at[pl.ds(HD, HD)], in_sem.at[2]),
        pltpu.make_async_copy(gain, gbuf, in_sem.at[3]),
    ]
    big = [pltpu.make_async_copy(ctx.at[v], xbuf.at[v], x_sem.at[v]) for v in range(videos)]
    for copy in small:
        copy.start()
    big[0].start()
    barrier = pltpu.get_barrier_semaphore()
    for k in reversed(OFFSETS[1:]):
        pl.semaphore_signal(barrier, inc=1, device_id={"tok": at(k), "head": head}, device_id_type=MESH)
    for i in range(1, 8):
        pl.semaphore_signal(barrier, inc=1, device_id={"tok": tok, "head": (head + i) % 8}, device_id_type=MESH)
    for copy in big[1:]:
        copy.start()
    own_w = pltpu.make_async_copy(out_w, wr.at[head], w_own)
    own_w.start()

    for copy in small:
        copy.wait()
    row = qin[...].astype(jnp.float32) * HD**-0.5
    row = jnp.concatenate([jnp.zeros((1, HD), jnp.float32), row], axis=1)
    qs[0] = row
    qr[0] = row
    w[...] = wt[...].T

    for v in range(videos):
        big[v].wait()
        data = xbuf[v].astype(jnp.float32)
        meansq = jnp.mean(data * data, axis=-1, keepdims=True)
        normed[...] = (data * lax.rsqrt(meansq + 1e-06) * gbuf[...]).astype(jnp.bfloat16)
        kv[v] = jnp.dot(normed[...], w[...], preferred_element_type=jnp.float32).astype(jnp.bfloat16)

    pl.semaphore_wait(barrier, N - 1 + 7)
    for j in reversed(range(1, N)):
        pltpu.make_async_remote_copy(
            src_ref=qs.at[0], dst_ref=qr.at[j], send_sem=q_send, recv_sem=q_recv.at[j // GROUP],
            device_id={"tok": at(OFFSETS[j]), "head": head}, device_id_type=MESH,
        ).start()
    for i in range(1, 8):
        pltpu.make_async_remote_copy(
            src_ref=out_w, dst_ref=wr.at[head], send_sem=w_send, recv_sem=w_recv,
            device_id={"tok": tok, "head": (head + i) % 8}, device_id_type=MESH,
        ).start()

    lane = lax.broadcasted_iota(jnp.int32, (GROUP, 2 * HD), 1)
    for g in range(N // GROUP):
        first = max(g * GROUP, 1)
        came = qr.at[pl.ds(first, (g + 1) * GROUP - first)]
        pltpu.make_async_copy(came, came, q_recv.at[g]).wait()
        rows = pl.ds(g * GROUP, GROUP)
        qg = qr[rows].reshape(GROUP, 2 * HD).astype(jnp.bfloat16)
        for v in range(videos):
            scores = lax.dot_general(qg, kv[v], (((1,), (1,)), ((), ())), preferred_element_type=jnp.float32)
            top = jnp.max(scores, axis=-1, keepdims=True)
            expo = jnp.exp(scores - top)
            total = jnp.sum(expo, axis=-1, keepdims=True)
            acc = jnp.dot(expo.astype(jnp.bfloat16), kv[v], preferred_element_type=jnp.float32)
            ps[rows, v, :] = jnp.where(lane < HD, acc, jnp.where(lane == HD, top, total))
        for j in range(g * GROUP, (g + 1) * GROUP):
            if j < N - 1:
                pltpu.make_async_remote_copy(
                    src_ref=ps.at[j], dst_ref=pr.at[j], send_sem=p_send, recv_sem=p_recv,
                    device_id={"tok": at(opposite(OFFSETS[j])), "head": head}, device_id_type=MESH,
                ).start()
            else:
                pr[j] = ps[j]

    came = pr.at[pl.ds(0, N - 1)]
    pltpu.make_async_copy(came, came, p_recv).wait()
    parts = pr[...]
    top = jnp.max(parts, axis=0)
    factor = jnp.exp(parts - top[None])[:, :, HD : HD + 1]
    joined = jnp.sum(parts * factor, axis=0)
    att[...] = joined / joined[:, HD + 1 : HD + 2]

    mine = ((yh + 1) % 2) * 4 + (x + 2) % 4
    slot = (z + 4) % 8
    for j in reversed(range(1, N)):
        pltpu.make_async_remote_copy(
            src_ref=att, dst_ref=ar.at[head, slot], send_sem=a_send, recv_sem=a_recv,
            device_id={"tok": at(OFFSETS[j]), "head": mine}, device_id_type=MESH,
        ).start()

    @pl.when(mine != head)
    def _():
        pltpu.make_async_remote_copy(
            src_ref=att, dst_ref=ar.at[head, slot], send_sem=a_send, recv_sem=a_recv,
            device_id={"tok": tok, "head": mine}, device_id_type=MESH,
        ).start()

    @pl.when(mine == head)
    def _():
        pltpu.make_async_copy(att, ar.at[head, slot], a_recv).start()

    own_w.wait()
    pltpu.make_async_copy(wr.at[pl.ds(0, 7)], wr.at[pl.ds(0, 7)], w_recv).wait()
    pltpu.make_async_copy(wr.at[pl.ds(0, 7)], wr.at[pl.ds(0, 7)], w_send).wait()
    gone = qr.at[pl.ds(0, N - 1)]
    pltpu.make_async_copy(gone, gone, q_send).wait()
    gone = ps.at[pl.ds(0, N - 1)]
    pltpu.make_async_copy(gone, gone, p_send).wait()

    pltpu.make_async_copy(ar, ar, a_recv).wait()
    result = jnp.zeros((64, HD), jnp.float32)
    for h in range(8):
        attended = ar[h].reshape(64, 2 * HD)[:, :HD].astype(jnp.bfloat16)
        result += jnp.dot(attended, wr[h], preferred_element_type=jnp.float32)
    out[...] = result.reshape(out.shape).astype(out.dtype)

    pltpu.make_async_copy(gone, gone, a_send).wait()

    @pl.when(mine != head)
    def _():
        pltpu.make_async_copy(att, att, a_send).wait()


def per_device(context, ctx_gain, queries, key_weight, value_weight, out_weight):
    videos, tokens, width = context.shape
    f32, bf16 = jnp.float32, jnp.bfloat16
    anywhere = pl.BlockSpec(memory_space=pl.ANY)
    dma = pltpu.SemaphoreType.DMA
    return pl.pallas_call(
        kernel,
        out_shape=jax.ShapeDtypeStruct((8, videos, out_weight.shape[1]), bf16),
        in_specs=[anywhere] * 6,
        out_specs=pl.BlockSpec(memory_space=pltpu.VMEM),
        scratch_shapes=[
            pltpu.VMEM((videos, tokens, width), bf16),
            pltpu.VMEM((1, width), f32),
            pltpu.VMEM((1, HD), bf16),
            pltpu.VMEM((2 * HD, width), bf16),
            pltpu.VMEM((width, 2 * HD), bf16),
            pltpu.VMEM((tokens, width), bf16),
            pltpu.VMEM((videos, tokens, 2 * HD), bf16),
            pltpu.VMEM((1, 1, 2 * HD), f32),
            pltpu.VMEM((N, 1, 2 * HD), f32),
            pltpu.VMEM((N, videos, 2 * HD), f32),
            pltpu.VMEM((N, videos, 2 * HD), f32),
            pltpu.VMEM((videos, 2 * HD), f32),
            pltpu.VMEM((8, 8, videos, 2 * HD), f32),
            pltpu.VMEM((8, HD, out_weight.shape[1]), bf16),
            dma((4,)), dma((videos,)),
            dma, dma((N // GROUP,)), dma, dma, dma, dma, dma, dma, dma,
        ],
        compiler_params=pltpu.CompilerParams(
            collective_id=0, has_side_effects=True, vmem_limit_bytes=40 * 2**20
        ),
        name="resampler",
    )(context, ctx_gain.reshape(1, width), queries, key_weight.T, value_weight.T, out_weight)


def solution(mesh):
    in_specs = (
        P(None, "tok", None),
        P(),
        P("tok", "head"),
        P(None, "head"),
        P(None, "head"),
        P("head", "tok"),
    )
    out_specs = P("head", None, "tok")
    return jax.shard_map(per_device, mesh=mesh, in_specs=in_specs, out_specs=out_specs, check_vma=False)
```

```python
import functools

import jax
import jax.numpy as jnp
from jax import lax
from jax.experimental import pallas as pl
from jax.experimental.pallas import tpu as pltpu
from jax.sharding import PartitionSpec as P

MESH = pl.DeviceIdType.MESH
HD = 64
GROUP = 16
HALF = 4
RING = (2, 4, 8)
HOPS = (4, 1, 1)
OPPOSITE = (1, 2, 4)


def distance(k):
    return sum(min(a, n - a) * w for a, n, w in zip(k, RING, HOPS))


def opposite(k):
    return tuple((o - a) % n for o, a, n in zip(OPPOSITE, k, RING))


def ordered_offsets():
    every = [(a, b, c) for a in range(2) for b in range(4) for c in range(8)]
    half = []
    for k in sorted(every, key=lambda k: (distance(k), k)):
        if len(half) < 32 and opposite(k) not in half:
            half.append(k)
    return half + [opposite(k) for k in reversed(half)]


OFFSETS = ordered_offsets()
N = len(OFFSETS)


def kernel(
    ctx, gain, query, key_t, value_t, out_w, out,
    xbuf, gbuf, qin, wt, w, normed, kv, qs, qr, ps, pr, att, ar, wr, wd,
    in_sem, x_sem, q_send, q_recv, p_send, p_recv, a_send, a_recv, w_send, w_recv, w_own,
):
    tok, head = lax.axis_index("tok"), lax.axis_index("head")
    yh, x, z = tok // 32, (tok // 8) % 4, tok % 8
    ys = [((yh + a) % 2) * 32 for a in range(2)]
    xs = [((x + a) % 4) * 8 for a in range(4)]
    zs = [(z + a) % 8 for a in range(8)]

    def at(k):
        return ys[k[0]] + xs[k[1]] + zs[k[2]]

    videos = ctx.shape[0]
    small = [
        pltpu.make_async_copy(query, qin, in_sem.at[0]),
        pltpu.make_async_copy(value_t, wt.at[0], in_sem.at[1]),
        pltpu.make_async_copy(key_t, wt.at[1], in_sem.at[2]),
        pltpu.make_async_copy(gain, gbuf, in_sem.at[3]),
    ]
    big = [pltpu.make_async_copy(ctx.at[v], xbuf.at[v], x_sem.at[v]) for v in range(videos)]
    for copy in small:
        copy.start()
    big[0].start()
    barrier = pltpu.get_barrier_semaphore()
    for k in reversed(OFFSETS[1:]):
        pl.semaphore_signal(barrier, inc=1, device_id={"tok": at(k), "head": head}, device_id_type=MESH)
    for i in range(1, 8):
        pl.semaphore_signal(barrier, inc=1, device_id={"tok": tok, "head": (head + i) % 8}, device_id_type=MESH)
    for copy in big[1:]:
        copy.start()
    own_w = pltpu.make_async_copy(out_w, wr.at[head], w_own)
    own_w.start()

    for copy in small:
        copy.wait()
    row = qin[...].astype(jnp.float32) * HD**-0.5
    row = jnp.concatenate([jnp.zeros((1, HD), jnp.float32), row], axis=1)
    qs[0] = row
    qr[0] = row
    value_w, key_w = wt[0].T, wt[1].T
    w[0] = jnp.concatenate([value_w, key_w], axis=1)
    w[1] = jnp.concatenate([key_w, value_w], axis=1)

    for v in range(videos):
        big[v].wait()
        data = xbuf[v].astype(jnp.float32)
        meansq = jnp.mean(data * data, axis=-1, keepdims=True)
        normed[...] = (data * lax.rsqrt(meansq + 1e-06) * gbuf[...]).astype(jnp.bfloat16)
        kv[v] = jnp.dot(normed[...], w[v // HALF], preferred_element_type=jnp.float32).astype(jnp.bfloat16)

    pl.semaphore_wait(barrier, N - 1 + 7)
    for j in reversed(range(1, N)):
        pltpu.make_async_remote_copy(
            src_ref=qs.at[0], dst_ref=qr.at[j], send_sem=q_send, recv_sem=q_recv.at[j // GROUP],
            device_id={"tok": at(OFFSETS[j]), "head": head}, device_id_type=MESH,
        ).start()
    for i in range(1, 8):
        pltpu.make_async_remote_copy(
            src_ref=out_w, dst_ref=wr.at[head], send_sem=w_send, recv_sem=w_recv,
            device_id={"tok": tok, "head": (head + i) % 8}, device_id_type=MESH,
        ).start()

    lane = lax.broadcasted_iota(jnp.int32, (GROUP, 2 * HD), 1)
    for g in range(N // GROUP):
        first = max(g * GROUP, 1)
        came = qr.at[pl.ds(first, (g + 1) * GROUP - first)]
        pltpu.make_async_copy(came, came, q_recv.at[g]).wait()
        rows = pl.ds(g * GROUP, GROUP)
        qg = qr[rows].reshape(GROUP, 2 * HD)
        qs_of = [qg.astype(jnp.bfloat16), pltpu.roll(qg, HD, 1).astype(jnp.bfloat16)]
        accs, stats = [], jnp.zeros((GROUP, 2 * HD), jnp.float32)
        for v in range(videos):
            scores = lax.dot_general(
                qs_of[v // HALF], kv[v], (((1,), (1,)), ((), ())), preferred_element_type=jnp.float32
            )
            top = jnp.max(scores, axis=-1, keepdims=True)
            expo = jnp.exp(scores - top)
            total = jnp.sum(expo, axis=-1, keepdims=True)
            accs.append(jnp.dot(expo.astype(jnp.bfloat16), kv[v], preferred_element_type=jnp.float32))
            stats = jnp.where(lane == v, top, jnp.where(lane == videos + v, total, stats))
        for i in range(HALF):
            ps[rows, i, :] = jnp.where(lane < HD, accs[i], accs[i + HALF])
        ps[rows, HALF, :] = stats
        for j in range(g * GROUP, (g + 1) * GROUP):
            if j < N - 1:
                pltpu.make_async_remote_copy(
                    src_ref=ps.at[j], dst_ref=pr.at[j], send_sem=p_send, recv_sem=p_recv,
                    device_id={"tok": at(opposite(OFFSETS[j])), "head": head}, device_id_type=MESH,
                ).start()
            else:
                pr[j] = ps[j]

    own_w.wait()
    pltpu.make_async_copy(wr.at[pl.ds(0, 7)], wr.at[pl.ds(0, 7)], w_recv).wait()
    zeros = jnp.zeros((HD, HD), jnp.bfloat16)
    for h in range(8):
        wide = jnp.concatenate([wr[h], zeros], axis=1)
        wd[pl.ds(2 * HD * h, HD)] = wide
        wide = jnp.concatenate([zeros, wr[h]], axis=1)
        wd[pl.ds(2 * HD * h + HD, HD)] = wide

    came = pr.at[pl.ds(0, N - 1)]
    pltpu.make_async_copy(came, came, p_recv).wait()
    stats = pr[:, HALF, :]
    low = lax.broadcasted_iota(jnp.int32, (1, 2 * HD), 1) < HD
    factor = jnp.exp(stats - jnp.max(stats, axis=0, keepdims=True))
    total = jnp.sum(factor * pltpu.roll(stats, 2 * HD - videos, 1), axis=0, keepdims=True)
    attended = []
    for i in range(HALF):
        weight = jnp.where(low, factor[:, i : i + 1], factor[:, i + HALF : i + HALF + 1])
        accum = jnp.sum(weight * pr[:, i, :], axis=0, keepdims=True)
        attended.append(accum / jnp.where(low, total[:, i : i + 1], total[:, i + HALF : i + HALF + 1]))
    att[...] = jnp.concatenate(attended, axis=0).astype(att.dtype)

    mine = ((yh + 1) % 2) * 4 + (x + 2) % 4
    slot = (z + 4) % 8
    for j in reversed(range(1, N)):
        pltpu.make_async_remote_copy(
            src_ref=att, dst_ref=ar.at[head, slot], send_sem=a_send, recv_sem=a_recv,
            device_id={"tok": at(OFFSETS[j]), "head": mine}, device_id_type=MESH,
        ).start()

    @pl.when(mine != head)
    def _():
        pltpu.make_async_remote_copy(
            src_ref=att, dst_ref=ar.at[head, slot], send_sem=a_send, recv_sem=a_recv,
            device_id={"tok": tok, "head": mine}, device_id_type=MESH,
        ).start()

    @pl.when(mine == head)
    def _():
        pltpu.make_async_copy(att, ar.at[head, slot], a_recv).start()

    pltpu.make_async_copy(wr.at[pl.ds(0, 7)], wr.at[pl.ds(0, 7)], w_send).wait()
    gone = qr.at[pl.ds(0, N - 1)]
    pltpu.make_async_copy(gone, gone, q_send).wait()
    gone = ps.at[pl.ds(0, N - 1)]
    pltpu.make_async_copy(gone, gone, p_send).wait()

    pltpu.make_async_copy(ar, ar, a_recv).wait()
    blocks = [ar[h].astype(jnp.float32).reshape(8 * HALF, 2 * HD).astype(jnp.bfloat16) for h in range(8)]
    result = jnp.dot(jnp.concatenate(blocks, axis=1), wd[...], preferred_element_type=jnp.float32)
    result = result.reshape(8, HALF, 2 * HD)
    out[...] = jnp.concatenate([result[:, :, :HD], result[:, :, HD:]], axis=1).astype(out.dtype)

    gone = ar.at[0, pl.ds(0, 7)]
    for _ in range(9):
        pltpu.make_async_copy(gone, gone, a_send).wait()

    @pl.when(mine != head)
    def _():
        pltpu.make_async_copy(att, att, a_send).wait()


def per_device(context, ctx_gain, queries, key_weight, value_weight, out_weight):
    videos, tokens, width = context.shape
    f32, bf16 = jnp.float32, jnp.bfloat16
    anywhere = pl.BlockSpec(memory_space=pl.ANY)
    dma = pltpu.SemaphoreType.DMA
    return pl.pallas_call(
        kernel,
        out_shape=jax.ShapeDtypeStruct((8, videos, out_weight.shape[1]), bf16),
        in_specs=[anywhere] * 6,
        out_specs=pl.BlockSpec(memory_space=pltpu.VMEM),
        scratch_shapes=[
            pltpu.VMEM((videos, tokens, width), bf16),
            pltpu.VMEM((1, width), f32),
            pltpu.VMEM((1, HD), bf16),
            pltpu.VMEM((2, HD, width), bf16),
            pltpu.VMEM((2, width, 2 * HD), bf16),
            pltpu.VMEM((tokens, width), bf16),
            pltpu.VMEM((videos, tokens, 2 * HD), bf16),
            pltpu.VMEM((1, 1, 2 * HD), f32),
            pltpu.VMEM((N, 1, 2 * HD), f32),
            pltpu.VMEM((N, HALF + 1, 2 * HD), f32),
            pltpu.VMEM((N, HALF + 1, 2 * HD), f32),
            pltpu.VMEM((HALF, 2 * HD), bf16),
            pltpu.VMEM((8, 8, HALF, 2 * HD), bf16),
            pltpu.VMEM((8, HD, out_weight.shape[1]), bf16),
            pltpu.VMEM((8 * 2 * HD, 2 * HD), bf16),
            dma((4,)), dma((videos,)),
            dma, dma((N // GROUP,)), dma, dma, dma, dma, dma, dma, dma,
        ],
        compiler_params=pltpu.CompilerParams(
            collective_id=0, has_side_effects=True, vmem_limit_bytes=60 * 2**20
        ),
        name="resampler",
    )(context, ctx_gain.reshape(1, width), queries, key_weight.T, value_weight.T, out_weight)


def solution(mesh):
    in_specs = (
        P(None, "tok", None),
        P(),
        P("tok", "head"),
        P(None, "head"),
        P(None, "head"),
        P("head", "tok"),
    )
    out_specs = P("head", None, "tok")
    return jax.shard_map(per_device, mesh=mesh, in_specs=in_specs, out_specs=out_specs, check_vma=False)
```

```python
import functools

import jax
import jax.numpy as jnp
from jax import lax
from jax.experimental import pallas as pl
from jax.experimental.pallas import tpu as pltpu
from jax.sharding import PartitionSpec as P

MESH = pl.DeviceIdType.MESH
HD = 64
GROUP = 8
HALF = 4
RING = (2, 4, 8)
HOPS = (4, 1, 1)
OPPOSITE = (1, 2, 4)


def distance(k):
    return sum(min(a, n - a) * w for a, n, w in zip(k, RING, HOPS))


def opposite(k):
    return tuple((o - a) % n for o, a, n in zip(OPPOSITE, k, RING))


def ordered_offsets():
    every = [(a, b, c) for a in range(2) for b in range(4) for c in range(8)]
    half = []
    for k in sorted(every, key=lambda k: (distance(k), k)):
        if len(half) < 32 and opposite(k) not in half:
            half.append(k)
    return half + [opposite(k) for k in reversed(half)]


OFFSETS = ordered_offsets()
N = len(OFFSETS)


def kernel(
    ctx, gain, query, key_t, value_t, out_w, out,
    xbuf, gbuf, qin, wt, normed, keys_t, values, qs, qr, ps, pr, att, ar, wr, wd,
    in_sem, x_sem, q_send, q_recv, p_send, p_recv, a_send, a_recv, w_send, w_recv, w_own,
):
    tok, head = lax.axis_index("tok"), lax.axis_index("head")
    yh, x, z = tok // 32, (tok // 8) % 4, tok % 8
    ys = [((yh + a) % 2) * 32 for a in range(2)]
    xs = [((x + a) % 4) * 8 for a in range(4)]
    zs = [(z + a) % 8 for a in range(8)]

    def at(k):
        return ys[k[0]] + xs[k[1]] + zs[k[2]]

    videos = ctx.shape[0]
    small = [
        pltpu.make_async_copy(query, qin, in_sem.at[0]),
        pltpu.make_async_copy(value_t, wt.at[0], in_sem.at[1]),
        pltpu.make_async_copy(key_t, wt.at[1], in_sem.at[2]),
        pltpu.make_async_copy(gain, gbuf, in_sem.at[3]),
    ]
    big = [pltpu.make_async_copy(ctx.at[v], xbuf.at[v], x_sem.at[v]) for v in range(videos)]
    for copy in small:
        copy.start()
    big[0].start()
    barrier = pltpu.get_barrier_semaphore()
    for k in reversed(OFFSETS[1:]):
        pl.semaphore_signal(barrier, inc=1, device_id={"tok": at(k), "head": head}, device_id_type=MESH)
    for i in range(1, 8):
        pl.semaphore_signal(barrier, inc=1, device_id={"tok": tok, "head": (head + i) % 8}, device_id_type=MESH)
    for copy in big[1:]:
        copy.start()
    own_w = pltpu.make_async_copy(out_w, wr.at[head], w_own)
    own_w.start()

    for copy in small:
        copy.wait()
    row = qin[...].astype(jnp.float32) * HD**-0.5
    row = jnp.concatenate([row, row], axis=1)
    qs[0] = row
    qr[0] = row

    key_value = jnp.concatenate([wt[1], wt[0]], axis=0)
    value_key = jnp.concatenate([wt[0], wt[1]], axis=0)
    low = lax.broadcasted_iota(jnp.int32, (xbuf.shape[1], 2 * HD), 1) < HD

    def project(v, weights):
        big[v].wait()
        data = xbuf[v].astype(jnp.float32)
        meansq = jnp.mean(data * data, axis=-1, keepdims=True)
        normed[v] = (data * lax.rsqrt(meansq + 1e-06) * gbuf[...]).astype(jnp.bfloat16)
        return lax.dot_general(
            normed[v], weights, (((1,), (1,)), ((), ())), preferred_element_type=jnp.float32
        )

    for i in range(HALF):
        first, second = project(i, key_value), project(i + HALF, value_key)
        keys_t[i] = jnp.where(low, first, second).astype(jnp.bfloat16).T
        values[i] = jnp.where(low, second, first).astype(jnp.bfloat16)

    pl.semaphore_wait(barrier, N - 1 + 7)
    for j in reversed(range(1, N)):
        pltpu.make_async_remote_copy(
            src_ref=qs.at[0], dst_ref=qr.at[j], send_sem=q_send, recv_sem=q_recv.at[j // GROUP],
            device_id={"tok": at(OFFSETS[j]), "head": head}, device_id_type=MESH,
        ).start()
    for i in range(1, 8):
        pltpu.make_async_remote_copy(
            src_ref=out_w, dst_ref=wr.at[head], send_sem=w_send, recv_sem=w_recv,
            device_id={"tok": tok, "head": (head + i) % 8}, device_id_type=MESH,
        ).start()

    lane = lax.broadcasted_iota(jnp.int32, (GROUP, 2 * HD), 1)
    all_keys_t = keys_t[...].reshape(HALF * 2 * HD, xbuf.shape[1])
    all_values = jnp.concatenate([values[i] for i in range(HALF)], axis=1)
    for g in range(N // GROUP):
        first = max(g * GROUP, 1)
        came = qr.at[pl.ds(first, (g + 1) * GROUP - first)]
        pltpu.make_async_copy(came, came, q_recv.at[g]).wait()
        rows = pl.ds(g * GROUP, GROUP)
        both = qr[rows].reshape(GROUP, 2 * HD)
        left, right = jnp.where(lane < HD, both, 0.0), jnp.where(lane < HD, 0.0, both)
        none = jnp.zeros_like(both)
        spread = jnp.concatenate(
            [
                jnp.concatenate(
                    [(left if v < HALF else right) if v % HALF == i else none for v in range(videos)], axis=0
                )
                for i in range(HALF)
            ],
            axis=1,
        ).astype(jnp.bfloat16)
        scores = jnp.dot(spread, all_keys_t, preferred_element_type=jnp.float32)
        top = jnp.max(scores, axis=-1, keepdims=True)
        expo = jnp.exp(scores - top)
        total = jnp.sum(expo, axis=-1, keepdims=True)
        acc = jnp.dot(expo.astype(jnp.bfloat16), all_values, preferred_element_type=jnp.float32)
        stats = jnp.zeros((GROUP, 2 * HD), jnp.float32)
        for v in range(videos):
            own = slice(v * GROUP, (v + 1) * GROUP)
            stats = jnp.where(lane == v, top[own], jnp.where(lane == videos + v, total[own], stats))
        for i in range(HALF):
            lanes = slice(2 * HD * i, 2 * HD * (i + 1))
            low_rows = slice((i + HALF) * GROUP, (i + HALF + 1) * GROUP)
            high_rows = slice(i * GROUP, (i + 1) * GROUP)
            ps[rows, i, :] = jnp.where(lane < HD, acc[low_rows, lanes], acc[high_rows, lanes])
        ps[rows, HALF, :] = stats
        for j in range(g * GROUP, (g + 1) * GROUP):
            if j < N - 1:
                pltpu.make_async_remote_copy(
                    src_ref=ps.at[j], dst_ref=pr.at[j], send_sem=p_send, recv_sem=p_recv,
                    device_id={"tok": at(opposite(OFFSETS[j])), "head": head}, device_id_type=MESH,
                ).start()
            else:
                pr[j] = ps[j]

    own_w.wait()
    pltpu.make_async_copy(wr.at[pl.ds(0, 7)], wr.at[pl.ds(0, 7)], w_recv).wait()
    zeros = jnp.zeros((HD, HD), jnp.bfloat16)
    for h in range(8):
        wide = jnp.concatenate([zeros, wr[h]], axis=1)
        wd[pl.ds(2 * HD * h, HD)] = wide
        wide = jnp.concatenate([wr[h], zeros], axis=1)
        wd[pl.ds(2 * HD * h + HD, HD)] = wide

    came = pr.at[pl.ds(0, N - 1)]
    pltpu.make_async_copy(came, came, p_recv).wait()
    stats = pr[:, HALF, :]
    low = lax.broadcasted_iota(jnp.int32, (1, 2 * HD), 1) < HD
    factor = jnp.exp(stats - jnp.max(stats, axis=0, keepdims=True))
    total = jnp.sum(factor * pltpu.roll(stats, 2 * HD - videos, 1), axis=0, keepdims=True)
    attended = []
    for i in range(HALF):
        weight = jnp.where(low, factor[:, i + HALF : i + HALF + 1], factor[:, i : i + 1])
        accum = jnp.sum(weight * pr[:, i, :], axis=0, keepdims=True)
        attended.append(accum / jnp.where(low, total[:, i + HALF : i + HALF + 1], total[:, i : i + 1]))
    att[...] = jnp.concatenate(attended, axis=0).astype(att.dtype)

    mine = ((yh + 1) % 2) * 4 + (x + 2) % 4
    slot = (z + 4) % 8
    for j in reversed(range(1, N)):
        pltpu.make_async_remote_copy(
            src_ref=att, dst_ref=ar.at[head, slot], send_sem=a_send, recv_sem=a_recv,
            device_id={"tok": at(OFFSETS[j]), "head": mine}, device_id_type=MESH,
        ).start()

    @pl.when(mine != head)
    def _():
        pltpu.make_async_remote_copy(
            src_ref=att, dst_ref=ar.at[head, slot], send_sem=a_send, recv_sem=a_recv,
            device_id={"tok": tok, "head": mine}, device_id_type=MESH,
        ).start()

    @pl.when(mine == head)
    def _():
        pltpu.make_async_copy(att, ar.at[head, slot], a_recv).start()

    pltpu.make_async_copy(wr.at[pl.ds(0, 7)], wr.at[pl.ds(0, 7)], w_send).wait()
    gone = qr.at[pl.ds(0, N - 1)]
    pltpu.make_async_copy(gone, gone, q_send).wait()
    gone = ps.at[pl.ds(0, N - 1)]
    pltpu.make_async_copy(gone, gone, p_send).wait()

    pltpu.make_async_copy(ar, ar, a_recv).wait()
    blocks = [ar[h].astype(jnp.float32).reshape(8 * HALF, 2 * HD).astype(jnp.bfloat16) for h in range(8)]
    result = jnp.dot(jnp.concatenate(blocks, axis=1), wd[...], preferred_element_type=jnp.float32)
    result = result.reshape(8, HALF, 2 * HD)
    out[...] = jnp.concatenate([result[:, :, :HD], result[:, :, HD:]], axis=1).astype(out.dtype)

    gone = ar.at[0, pl.ds(0, 7)]
    for _ in range(9):
        pltpu.make_async_copy(gone, gone, a_send).wait()

    @pl.when(mine != head)
    def _():
        pltpu.make_async_copy(att, att, a_send).wait()


def per_device(context, ctx_gain, queries, key_weight, value_weight, out_weight):
    videos, tokens, width = context.shape
    f32, bf16 = jnp.float32, jnp.bfloat16
    anywhere = pl.BlockSpec(memory_space=pl.ANY)
    dma = pltpu.SemaphoreType.DMA
    return pl.pallas_call(
        kernel,
        out_shape=pltpu.VMEM((8, videos, out_weight.shape[1]), bf16),
        in_specs=[anywhere] * 6,
        out_specs=pl.BlockSpec(memory_space=pltpu.VMEM),
        scratch_shapes=[
            pltpu.VMEM((videos, tokens, width), bf16),
            pltpu.VMEM((1, width), f32),
            pltpu.VMEM((1, HD), bf16),
            pltpu.VMEM((2, HD, width), bf16),
            pltpu.VMEM((videos, tokens, width), bf16),
            pltpu.VMEM((HALF, 2 * HD, tokens), bf16),
            pltpu.VMEM((HALF, tokens, 2 * HD), bf16),
            pltpu.VMEM((1, 1, 2 * HD), f32),
            pltpu.VMEM((N, 1, 2 * HD), f32),
            pltpu.VMEM((N, HALF + 1, 2 * HD), f32),
            pltpu.VMEM((N, HALF + 1, 2 * HD), f32),
            pltpu.VMEM((HALF, 2 * HD), bf16),
            pltpu.VMEM((8, 8, HALF, 2 * HD), bf16),
            pltpu.VMEM((8, HD, out_weight.shape[1]), bf16),
            pltpu.VMEM((8 * 2 * HD, 2 * HD), bf16),
            dma((4,)), dma((videos,)),
            dma, dma((N // GROUP,)), dma, dma, dma, dma, dma, dma, dma,
        ],
        compiler_params=pltpu.CompilerParams(
            collective_id=0, has_side_effects=True, vmem_limit_bytes=60 * 2**20
        ),
        name="resampler",
    )(context, ctx_gain.reshape(1, width), queries, key_weight.T, value_weight.T, out_weight)


def solution(mesh):
    in_specs = (
        P(None, "tok", None),
        P(),
        P("tok", "head"),
        P(None, "head"),
        P(None, "head"),
        P("head", "tok"),
    )
    out_specs = P("head", None, "tok")
    return jax.shard_map(per_device, mesh=mesh, in_specs=in_specs, out_specs=out_specs, check_vma=False)
```

```python
import functools

import jax
import jax.numpy as jnp
from jax import lax
from jax.experimental import pallas as pl
from jax.experimental.pallas import tpu as pltpu
from jax.sharding import PartitionSpec as P

MESH = pl.DeviceIdType.MESH
HD = 64
GROUP = 8
HALF = 4
RING = (2, 4, 8)
HOPS = (4, 1, 1)
OPPOSITE = (1, 2, 4)


def distance(k):
    return sum(min(a, n - a) * w for a, n, w in zip(k, RING, HOPS))


def opposite(k):
    return tuple((o - a) % n for o, a, n in zip(OPPOSITE, k, RING))


EVERY = [(a, b, c) for a in range(2) for b in range(4) for c in range(8)]
RANKS = [[k for k in EVERY if distance(k) == d] for d in range(11)]
OFFSETS = [k for rank in RANKS for k in rank]
SLOTS = [GROUP * d + i for d, rank in enumerate(RANKS) for i in range(len(rank))]
N = len(OFFSETS)


def kernel(
    ctx, gain, query, key_t, value_t, out_w, out,
    xbuf, gbuf, qin, wt, normed, keys_t, values, qs, qr, ps, pr, att, ar, wr, wd,
    in_sem, x_sem, q_send, q_recv, p_send, p_recv, a_send, a_recv, w_send, w_recv, w_own,
):
    tok, head = lax.axis_index("tok"), lax.axis_index("head")
    yh, x, z = tok // 32, (tok // 8) % 4, tok % 8
    ys = [((yh + a) % 2) * 32 for a in range(2)]
    xs = [((x + a) % 4) * 8 for a in range(4)]
    zs = [(z + a) % 8 for a in range(8)]

    def at(k):
        return ys[k[0]] + xs[k[1]] + zs[k[2]]

    videos = ctx.shape[0]
    small = [
        pltpu.make_async_copy(query, qin, in_sem.at[0]),
        pltpu.make_async_copy(value_t, wt.at[0], in_sem.at[1]),
        pltpu.make_async_copy(key_t, wt.at[1], in_sem.at[2]),
        pltpu.make_async_copy(gain, gbuf, in_sem.at[3]),
    ]
    big = [pltpu.make_async_copy(ctx.at[v], xbuf.at[v], x_sem.at[v]) for v in (0, 4, 1, 5, 2, 6, 3, 7)]
    barrier = pltpu.get_barrier_semaphore()
    for k in reversed(OFFSETS[1:]):
        pl.semaphore_signal(barrier, inc=1, device_id={"tok": at(k), "head": head}, device_id_type=MESH)
    for i in range(1, 8):
        pl.semaphore_signal(barrier, inc=1, device_id={"tok": tok, "head": (head + i) % 8}, device_id_type=MESH)
    for copy in small + big:
        copy.start()
    own_w = pltpu.make_async_copy(out_w, wr.at[head], w_own)
    own_w.start()

    for copy in small:
        copy.wait()
    row = qin[...].astype(jnp.float32) * HD**-0.5
    row = jnp.concatenate([row, row], axis=1)
    qs[0] = row
    qr[0] = row
    for i in range(GROUP * len(RANKS)):
        if i not in SLOTS:
            qr[i] = jnp.zeros_like(row)

    key_value = jnp.concatenate([wt[1], wt[0]], axis=0)
    value_key = jnp.concatenate([wt[0], wt[1]], axis=0)
    low = lax.broadcasted_iota(jnp.int32, (xbuf.shape[1], 2 * HD), 1) < HD

    def project(v, weights):
        pltpu.make_async_copy(ctx.at[v], xbuf.at[v], x_sem.at[v]).wait()
        data = xbuf[v].astype(jnp.float32)
        meansq = jnp.mean(data * data, axis=-1, keepdims=True)
        normed[v] = (data * lax.rsqrt(meansq + 1e-06) * gbuf[...]).astype(jnp.bfloat16)
        return lax.dot_general(
            normed[v], weights, (((1,), (1,)), ((), ())), preferred_element_type=jnp.float32
        )

    for i in range(HALF):
        first, second = project(i, key_value), project(i + HALF, value_key)
        keys_t[i] = jnp.where(low, first, second).astype(jnp.bfloat16).T
        values[i] = jnp.where(low, second, first).astype(jnp.bfloat16)

    lane = lax.broadcasted_iota(jnp.int32, (GROUP, 2 * HD), 1)
    all_keys_t = keys_t[...].reshape(HALF * 2 * HD, xbuf.shape[1])
    all_values = jnp.concatenate([values[i] for i in range(HALF)], axis=1)

    def score(d):
        rows = pl.ds(d * GROUP, GROUP)
        both = qr[rows].reshape(GROUP, 2 * HD)
        left, right = jnp.where(lane < HD, both, 0.0), jnp.where(lane < HD, 0.0, both)
        none = jnp.zeros_like(both)
        spread = jnp.concatenate(
            [
                jnp.concatenate(
                    [(left if v < HALF else right) if v % HALF == i else none for v in range(videos)], axis=0
                )
                for i in range(HALF)
            ],
            axis=1,
        ).astype(jnp.bfloat16)
        scores = jnp.dot(spread, all_keys_t, preferred_element_type=jnp.float32)
        top = jnp.max(scores, axis=-1, keepdims=True)
        expo = jnp.exp(scores - top)
        total = jnp.sum(expo, axis=-1, keepdims=True)
        acc = jnp.dot(expo.astype(jnp.bfloat16), all_values, preferred_element_type=jnp.float32)
        stats = jnp.zeros((GROUP, 2 * HD), jnp.float32)
        for v in range(videos):
            own = slice(v * GROUP, (v + 1) * GROUP)
            stats = jnp.where(lane == v, top[own], jnp.where(lane == videos + v, total[own], stats))
        for i in range(HALF):
            lanes = slice(2 * HD * i, 2 * HD * (i + 1))
            low_rows = slice((i + HALF) * GROUP, (i + HALF + 1) * GROUP)
            high_rows = slice(i * GROUP, (i + 1) * GROUP)
            ps[rows, i, :] = jnp.where(lane < HD, acc[low_rows, lanes], acc[high_rows, lanes])
        ps[rows, HALF, :] = stats

    score(0)
    pl.semaphore_wait(barrier, N - 1 + 7)
    for j in reversed(range(1, N)):
        pltpu.make_async_remote_copy(
            src_ref=qs.at[0], dst_ref=qr.at[SLOTS[j]], send_sem=q_send, recv_sem=q_recv.at[SLOTS[j] // GROUP],
            device_id={"tok": at(OFFSETS[j]), "head": head}, device_id_type=MESH,
        ).start()
    for i in range(1, 8):
        pltpu.make_async_remote_copy(
            src_ref=out_w, dst_ref=wr.at[head], send_sem=w_send, recv_sem=w_recv,
            device_id={"tok": tok, "head": (head + i) % 8}, device_id_type=MESH,
        ).start()


    for d, rank in enumerate(RANKS):
        if d > 0:
            came = qr.at[pl.ds(d * GROUP, len(rank))]
            pltpu.make_async_copy(came, came, q_recv.at[d]).wait()
            score(d)
        for k in rank:
            j = OFFSETS.index(k)
            if k == OPPOSITE:
                pr[j] = ps[SLOTS[j]]
            else:
                pltpu.make_async_remote_copy(
                    src_ref=ps.at[SLOTS[j]], dst_ref=pr.at[j], send_sem=p_send, recv_sem=p_recv,
                    device_id={"tok": at(opposite(k)), "head": head}, device_id_type=MESH,
                ).start()

    own_w.wait()
    pltpu.make_async_copy(wr.at[pl.ds(0, 7)], wr.at[pl.ds(0, 7)], w_recv).wait()
    zeros = jnp.zeros((HD, HD), jnp.bfloat16)
    for h in range(8):
        wide = jnp.concatenate([zeros, wr[h]], axis=1)
        wd[pl.ds(2 * HD * h, HD)] = wide
        wide = jnp.concatenate([wr[h], zeros], axis=1)
        wd[pl.ds(2 * HD * h + HD, HD)] = wide

    came = pr.at[pl.ds(0, N - 1)]
    pltpu.make_async_copy(came, came, p_recv).wait()
    stats = pr[:, HALF, :]
    low = lax.broadcasted_iota(jnp.int32, (1, 2 * HD), 1) < HD
    factor = jnp.exp(stats - jnp.max(stats, axis=0, keepdims=True))
    total = jnp.sum(factor * pltpu.roll(stats, 2 * HD - videos, 1), axis=0, keepdims=True)
    attended = []
    for i in range(HALF):
        weight = jnp.where(low, factor[:, i + HALF : i + HALF + 1], factor[:, i : i + 1])
        accum = jnp.sum(weight * pr[:, i, :], axis=0, keepdims=True)
        attended.append(accum / jnp.where(low, total[:, i + HALF : i + HALF + 1], total[:, i : i + 1]))
    att[...] = jnp.concatenate(attended, axis=0).astype(att.dtype)

    mine = ((yh + 1) % 2) * 4 + (x + 2) % 4
    slot = (z + 4) % 8
    for j in reversed(range(1, N)):
        pltpu.make_async_remote_copy(
            src_ref=att, dst_ref=ar.at[head, slot], send_sem=a_send, recv_sem=a_recv,
            device_id={"tok": at(OFFSETS[j]), "head": mine}, device_id_type=MESH,
        ).start()

    @pl.when(mine != head)
    def _():
        pltpu.make_async_remote_copy(
            src_ref=att, dst_ref=ar.at[head, slot], send_sem=a_send, recv_sem=a_recv,
            device_id={"tok": tok, "head": mine}, device_id_type=MESH,
        ).start()

    @pl.when(mine == head)
    def _():
        pltpu.make_async_copy(att, ar.at[head, slot], a_recv).start()

    pltpu.make_async_copy(wr.at[pl.ds(0, 7)], wr.at[pl.ds(0, 7)], w_send).wait()
    gone = qr.at[pl.ds(0, N - 1)]
    pltpu.make_async_copy(gone, gone, q_send).wait()
    gone = ps.at[pl.ds(0, N - 1)]
    pltpu.make_async_copy(gone, gone, p_send).wait()

    pltpu.make_async_copy(ar, ar, a_recv).wait()
    blocks = [ar[h].astype(jnp.float32).reshape(8 * HALF, 2 * HD).astype(jnp.bfloat16) for h in range(8)]
    result = jnp.dot(jnp.concatenate(blocks, axis=1), wd[...], preferred_element_type=jnp.float32)
    result = result.reshape(8, HALF, 2 * HD)
    out[...] = jnp.concatenate([result[:, :, :HD], result[:, :, HD:]], axis=1).astype(out.dtype)

    gone = ar.at[0, pl.ds(0, 7)]
    for _ in range(9):
        pltpu.make_async_copy(gone, gone, a_send).wait()

    @pl.when(mine != head)
    def _():
        pltpu.make_async_copy(att, att, a_send).wait()


def per_device(context, ctx_gain, queries, key_weight, value_weight, out_weight):
    videos, tokens, width = context.shape
    f32, bf16 = jnp.float32, jnp.bfloat16
    anywhere = pl.BlockSpec(memory_space=pl.ANY)
    dma = pltpu.SemaphoreType.DMA
    return pl.pallas_call(
        kernel,
        out_shape=pltpu.VMEM((8, videos, out_weight.shape[1]), bf16),
        in_specs=[anywhere] * 6,
        out_specs=pl.BlockSpec(memory_space=pltpu.VMEM),
        scratch_shapes=[
            pltpu.VMEM((videos, tokens, width), bf16),
            pltpu.VMEM((1, width), f32),
            pltpu.VMEM((1, HD), bf16),
            pltpu.VMEM((2, HD, width), bf16),
            pltpu.VMEM((videos, tokens, width), bf16),
            pltpu.VMEM((HALF, 2 * HD, tokens), bf16),
            pltpu.VMEM((HALF, tokens, 2 * HD), bf16),
            pltpu.VMEM((1, 1, 2 * HD), f32),
            pltpu.VMEM((GROUP * len(RANKS), 1, 2 * HD), f32),
            pltpu.VMEM((GROUP * len(RANKS), HALF + 1, 2 * HD), f32),
            pltpu.VMEM((N, HALF + 1, 2 * HD), f32),
            pltpu.VMEM((HALF, 2 * HD), bf16),
            pltpu.VMEM((8, 8, HALF, 2 * HD), bf16),
            pltpu.VMEM((8, HD, out_weight.shape[1]), bf16),
            pltpu.VMEM((8 * 2 * HD, 2 * HD), bf16),
            dma((4,)), dma((videos,)),
            dma, dma((len(RANKS),)), dma, dma, dma, dma, dma, dma, dma,
        ],
        compiler_params=pltpu.CompilerParams(
            collective_id=0, has_side_effects=True, vmem_limit_bytes=60 * 2**20
        ),
        name="resampler",
    )(context, ctx_gain.reshape(1, width), queries, key_weight.T, value_weight.T, out_weight)


def solution(mesh):
    in_specs = (
        P(None, "tok", None),
        P(),
        P("tok", "head"),
        P(None, "head"),
        P(None, "head"),
        P("head", "tok"),
    )
    out_specs = P("head", None, "tok")
    return jax.shard_map(per_device, mesh=mesh, in_specs=in_specs, out_specs=out_specs, check_vma=False)
```

```python
import functools

import jax
import jax.numpy as jnp
from jax import lax
from jax.experimental import pallas as pl
from jax.experimental.pallas import tpu as pltpu
from jax.sharding import PartitionSpec as P

MESH = pl.DeviceIdType.MESH
HD = 64
GROUP = 8
EARLY = 2
HALF = 4
RING = (2, 4, 8)
HOPS = (4, 1, 1)
OPPOSITE = (1, 2, 4)


def distance(k):
    return sum(min(a, n - a) * w for a, n, w in zip(k, RING, HOPS))


def opposite(k):
    return tuple((o - a) % n for o, a, n in zip(OPPOSITE, k, RING))


EVERY = [(a, b, c) for a in range(2) for b in range(4) for c in range(8)]
RANKS = [[k for k in EVERY if distance(k) == d] for d in range(11)]
OFFSETS = [k for rank in RANKS for k in rank]
SLOTS = [GROUP * d + i for d, rank in enumerate(RANKS) for i in range(len(rank))]
N = len(OFFSETS)


def kernel(
    ctx, gain, query, key_t, value_t, out_w, out,
    xbuf, gbuf, qin, wt, normed, keys_t, values, qs, qr, pf, ps, pr, ss, sr, wf, att, ar, wr, wd,
    in_sem, x_sem, q_send, q_recv, p_send, p_recv, s_send, s_recv, a_send, a_recv, w_send, w_recv, w_own,
):
    tok, head = lax.axis_index("tok"), lax.axis_index("head")
    yh, x, z = tok // 32, (tok // 8) % 4, tok % 8
    ys = [((yh + a) % 2) * 32 for a in range(2)]
    xs = [((x + a) % 4) * 8 for a in range(4)]
    zs = [(z + a) % 8 for a in range(8)]

    def at(k):
        return ys[k[0]] + xs[k[1]] + zs[k[2]]

    videos = ctx.shape[0]
    small = [
        pltpu.make_async_copy(query, qin, in_sem.at[0]),
        pltpu.make_async_copy(value_t, wt.at[0], in_sem.at[1]),
        pltpu.make_async_copy(key_t, wt.at[1], in_sem.at[2]),
        pltpu.make_async_copy(gain, gbuf, in_sem.at[3]),
    ]
    big = [pltpu.make_async_copy(ctx.at[v], xbuf.at[v], x_sem.at[v]) for v in (0, 4, 1, 5, 2, 6, 3, 7)]
    for copy in small + big:
        copy.start()
    own_w = pltpu.make_async_copy(out_w, wr.at[head], w_own)
    own_w.start()
    barrier = pltpu.get_barrier_semaphore()
    for k in reversed(OFFSETS[1:]):
        pl.semaphore_signal(barrier, inc=1, device_id={"tok": at(k), "head": head}, device_id_type=MESH)
    for i in range(1, 8):
        pl.semaphore_signal(barrier, inc=1, device_id={"tok": tok, "head": (head + i) % 8}, device_id_type=MESH)

    for copy in small:
        copy.wait()
    row = qin[...].astype(jnp.float32) * HD**-0.5
    row = jnp.concatenate([row, row], axis=1)
    qs[0] = row
    qr[0] = row
    for i in range(GROUP * len(RANKS)):
        if i not in SLOTS:
            qr[i] = jnp.zeros_like(row)

    key_value = jnp.concatenate([wt[1], wt[0]], axis=0)
    value_key = jnp.concatenate([wt[0], wt[1]], axis=0)
    low = lax.broadcasted_iota(jnp.int32, (xbuf.shape[1], 2 * HD), 1) < HD

    def project(v, weights):
        pltpu.make_async_copy(ctx.at[v], xbuf.at[v], x_sem.at[v]).wait()
        data = xbuf[v].astype(jnp.float32)
        meansq = jnp.mean(data * data, axis=-1, keepdims=True)
        normed[v] = (data * lax.rsqrt(meansq + 1e-06) * gbuf[...]).astype(jnp.bfloat16)
        return lax.dot_general(
            normed[v], weights, (((1,), (1,)), ((), ())), preferred_element_type=jnp.float32
        )

    def project_pairs(pairs):
        for i in pairs:
            first, second = project(i, key_value), project(i + HALF, value_key)
            keys_t[i] = jnp.where(low, first, second).astype(jnp.bfloat16).T
            values[i] = jnp.where(low, second, first).astype(jnp.bfloat16)

    project_pairs(range(EARLY))
    pl.semaphore_wait(barrier, N - 1 + 7)
    for j in reversed(range(1, N)):
        pltpu.make_async_remote_copy(
            src_ref=qs.at[0], dst_ref=qr.at[SLOTS[j]], send_sem=q_send, recv_sem=q_recv.at[SLOTS[j] // GROUP],
            device_id={"tok": at(OFFSETS[j]), "head": head}, device_id_type=MESH,
        ).start()
    for i in range(1, 8):
        pltpu.make_async_remote_copy(
            src_ref=out_w, dst_ref=wr.at[head], send_sem=w_send, recv_sem=w_recv,
            device_id={"tok": tok, "head": (head + i) % 8}, device_id_type=MESH,
        ).start()
    project_pairs(range(EARLY, HALF))

    lane = lax.broadcasted_iota(jnp.int32, (GROUP, 2 * HD), 1)
    all_keys_t = keys_t[...].reshape(HALF * 2 * HD, xbuf.shape[1])
    all_values = jnp.concatenate([values[i] for i in range(HALF)], axis=1)

    def score(d):
        rows = pl.ds(d * GROUP, GROUP)
        both = qr[rows].reshape(GROUP, 2 * HD)
        left, right = jnp.where(lane < HD, both, 0.0), jnp.where(lane < HD, 0.0, both)
        none = jnp.zeros_like(both)
        spread = jnp.concatenate(
            [
                jnp.concatenate(
                    [(left if v < HALF else right) if v % HALF == i else none for v in range(videos)], axis=0
                )
                for i in range(HALF)
            ],
            axis=1,
        ).astype(jnp.bfloat16)
        scores = jnp.dot(spread, all_keys_t, preferred_element_type=jnp.float32)
        top = jnp.max(scores, axis=-1, keepdims=True)
        expo = jnp.exp(scores - top)
        total = jnp.sum(expo, axis=-1, keepdims=True)
        acc = jnp.dot(expo.astype(jnp.bfloat16), all_values, preferred_element_type=jnp.float32)
        stats = jnp.zeros((GROUP, 2 * HD), jnp.float32)
        for v in range(videos):
            own = slice(v * GROUP, (v + 1) * GROUP)
            stats = jnp.where(lane == v, top[own], jnp.where(lane == videos + v, total[own], stats))
        for i in range(HALF):
            lanes = slice(2 * HD * i, 2 * HD * (i + 1))
            low_rows = slice((i + HALF) * GROUP, (i + HALF + 1) * GROUP)
            high_rows = slice(i * GROUP, (i + 1) * GROUP)
            pf[rows, i, :] = jnp.where(lane < HD, acc[low_rows, lanes], acc[high_rows, lanes])
        ps[rows] = pf[rows].astype(jnp.bfloat16)
        ss[rows] = stats.reshape(GROUP, 1, 2 * HD)

    score(0)
    for d, rank in enumerate(RANKS):
        if d > 0:
            came = qr.at[pl.ds(d * GROUP, len(rank))]
            pltpu.make_async_copy(came, came, q_recv.at[d]).wait()
            score(d)
        for k in rank:
            j = OFFSETS.index(k)
            if k == OPPOSITE:
                pr[j] = ps[SLOTS[j]]
                sr[j] = ss[SLOTS[j]]
            else:
                pltpu.make_async_remote_copy(
                    src_ref=ss.at[SLOTS[j]], dst_ref=sr.at[j], send_sem=s_send, recv_sem=s_recv,
                    device_id={"tok": at(opposite(k)), "head": head}, device_id_type=MESH,
                ).start()
                pltpu.make_async_remote_copy(
                    src_ref=ps.at[SLOTS[j]], dst_ref=pr.at[j], send_sem=p_send, recv_sem=p_recv,
                    device_id={"tok": at(opposite(k)), "head": head}, device_id_type=MESH,
                ).start()

    own_w.wait()
    pltpu.make_async_copy(wr.at[pl.ds(0, 7)], wr.at[pl.ds(0, 7)], w_recv).wait()
    zeros = jnp.zeros((HD, HD), jnp.bfloat16)
    for h in range(8):
        wide = jnp.concatenate([zeros, wr[h]], axis=1)
        wd[pl.ds(2 * HD * h, HD)] = wide
        wide = jnp.concatenate([wr[h], zeros], axis=1)
        wd[pl.ds(2 * HD * h + HD, HD)] = wide

    came = sr.at[pl.ds(0, N - 1)]
    pltpu.make_async_copy(came, came, s_recv).wait()
    stats = sr[...].reshape(N, 2 * HD)
    low = lax.broadcasted_iota(jnp.int32, (1, 2 * HD), 1) < HD
    factor = jnp.exp(stats - jnp.max(stats, axis=0, keepdims=True))
    total = jnp.sum(factor * pltpu.roll(stats, 2 * HD - videos, 1), axis=0, keepdims=True)
    totals = []
    for i in range(HALF):
        wf[:, i, :] = jnp.where(low, factor[:, i + HALF : i + HALF + 1], factor[:, i : i + 1])
        totals.append(jnp.where(low, total[:, i + HALF : i + HALF + 1], total[:, i : i + 1]))
    came = pr.at[pl.ds(0, N - 1)]
    pltpu.make_async_copy(came, came, p_recv).wait()
    accum = jnp.sum(wf[...] * pr[...].astype(jnp.float32), axis=0)
    att[...] = (accum / jnp.concatenate(totals, axis=0)).astype(att.dtype)

    mine = ((yh + 1) % 2) * 4 + (x + 2) % 4
    slot = (z + 4) % 8
    for j in reversed(range(1, N)):
        pltpu.make_async_remote_copy(
            src_ref=att, dst_ref=ar.at[head, slot], send_sem=a_send, recv_sem=a_recv,
            device_id={"tok": at(OFFSETS[j]), "head": mine}, device_id_type=MESH,
        ).start()

    @pl.when(mine != head)
    def _():
        pltpu.make_async_remote_copy(
            src_ref=att, dst_ref=ar.at[head, slot], send_sem=a_send, recv_sem=a_recv,
            device_id={"tok": tok, "head": mine}, device_id_type=MESH,
        ).start()

    @pl.when(mine == head)
    def _():
        pltpu.make_async_copy(att, ar.at[head, slot], a_recv).start()

    pltpu.make_async_copy(wr.at[pl.ds(0, 7)], wr.at[pl.ds(0, 7)], w_send).wait()
    gone = qr.at[pl.ds(0, N - 1)]
    pltpu.make_async_copy(gone, gone, q_send).wait()
    gone = ps.at[pl.ds(0, N - 1)]
    pltpu.make_async_copy(gone, gone, p_send).wait()
    gone = ss.at[pl.ds(0, N - 1)]
    pltpu.make_async_copy(gone, gone, s_send).wait()

    pltpu.make_async_copy(ar, ar, a_recv).wait()
    blocks = [ar[h].astype(jnp.float32).reshape(8 * HALF, 2 * HD).astype(jnp.bfloat16) for h in range(8)]
    result = jnp.dot(jnp.concatenate(blocks, axis=1), wd[...], preferred_element_type=jnp.float32)
    result = result.reshape(8, HALF, 2 * HD)
    out[...] = jnp.concatenate([result[:, :, :HD], result[:, :, HD:]], axis=1).astype(out.dtype)

    gone = ar.at[0, pl.ds(0, 7)]
    for _ in range(9):
        pltpu.make_async_copy(gone, gone, a_send).wait()

    @pl.when(mine != head)
    def _():
        pltpu.make_async_copy(att, att, a_send).wait()


def per_device(context, ctx_gain, queries, key_weight, value_weight, out_weight):
    videos, tokens, width = context.shape
    f32, bf16 = jnp.float32, jnp.bfloat16
    anywhere = pl.BlockSpec(memory_space=pl.ANY)
    dma = pltpu.SemaphoreType.DMA
    return pl.pallas_call(
        kernel,
        out_shape=pltpu.VMEM((8, videos, out_weight.shape[1]), bf16),
        in_specs=[anywhere] * 6,
        out_specs=pl.BlockSpec(memory_space=pltpu.VMEM),
        scratch_shapes=[
            pltpu.VMEM((videos, tokens, width), bf16),
            pltpu.VMEM((1, width), f32),
            pltpu.VMEM((1, HD), bf16),
            pltpu.VMEM((2, HD, width), bf16),
            pltpu.VMEM((videos, tokens, width), bf16),
            pltpu.VMEM((HALF, 2 * HD, tokens), bf16),
            pltpu.VMEM((HALF, tokens, 2 * HD), bf16),
            pltpu.VMEM((1, 1, 2 * HD), f32),
            pltpu.VMEM((GROUP * len(RANKS), 1, 2 * HD), f32),
            pltpu.VMEM((GROUP * len(RANKS), HALF, 2 * HD), f32),
            pltpu.VMEM((GROUP * len(RANKS), HALF, 2 * HD), bf16),
            pltpu.VMEM((N, HALF, 2 * HD), bf16),
            pltpu.VMEM((GROUP * len(RANKS), 1, 2 * HD), f32),
            pltpu.VMEM((N, 1, 2 * HD), f32),
            pltpu.VMEM((N, HALF, 2 * HD), f32),
            pltpu.VMEM((HALF, 2 * HD), bf16),
            pltpu.VMEM((8, 8, HALF, 2 * HD), bf16),
            pltpu.VMEM((8, HD, out_weight.shape[1]), bf16),
            pltpu.VMEM((8 * 2 * HD, 2 * HD), bf16),
            dma((4,)), dma((videos,)),
            dma, dma((len(RANKS),)), dma, dma, dma, dma, dma, dma, dma, dma, dma,
        ],
        compiler_params=pltpu.CompilerParams(
            collective_id=0, has_side_effects=True, vmem_limit_bytes=60 * 2**20
        ),
        name="resampler",
    )(context, ctx_gain.reshape(1, width), queries, key_weight.T, value_weight.T, out_weight)


def solution(mesh):
    in_specs = (
        P(None, "tok", None),
        P(),
        P("tok", "head"),
        P(None, "head"),
        P(None, "head"),
        P("head", "tok"),
    )
    out_specs = P("head", None, "tok")
    return jax.shard_map(per_device, mesh=mesh, in_specs=in_specs, out_specs=out_specs, check_vma=False)
```

```python
import functools

import jax
import jax.numpy as jnp
from jax import lax
from jax.experimental import pallas as pl
from jax.experimental.pallas import tpu as pltpu
from jax.sharding import PartitionSpec as P

MESH = pl.DeviceIdType.MESH
HD = 64
GROUP = 8
EARLY = 2
HALF = 4
RING = (2, 4, 8)
HOPS = (4, 1, 1)
OPPOSITE = (1, 2, 4)


def distance(k):
    return sum(min(a, n - a) * w for a, n, w in zip(k, RING, HOPS))


def opposite(k):
    return tuple((o - a) % n for o, a, n in zip(OPPOSITE, k, RING))


EVERY = [(a, b, c) for a in range(2) for b in range(4) for c in range(8)]
RANKS = [[k for k in EVERY if distance(k) == d] for d in range(11)]
OFFSETS = [k for rank in RANKS for k in rank]
RANKS = [OFFSETS[:1]] + [OFFSETS[i : i + GROUP] for i in range(1, len(OFFSETS), GROUP)]
SLOTS = [GROUP * d + i for d, rank in enumerate(RANKS) for i in range(len(rank))]
N = len(OFFSETS)


def kernel(
    ctx, gain, query, key_t, value_t, out_w, out,
    xbuf, gbuf, qin, wt, normed, keys_t, values, qs, qr, ps, pr, att, ar, wr, wd,
    in_sem, x_sem, q_send, q_recv, p_send, p_recv, a_send, a_recv, w_send, w_recv, w_own,
):
    tok, head = lax.axis_index("tok"), lax.axis_index("head")
    yh, x, z = tok // 32, (tok // 8) % 4, tok % 8
    ys = [((yh + a) % 2) * 32 for a in range(2)]
    xs = [((x + a) % 4) * 8 for a in range(4)]
    zs = [(z + a) % 8 for a in range(8)]

    def at(k):
        return ys[k[0]] + xs[k[1]] + zs[k[2]]

    videos = ctx.shape[0]
    small = [
        pltpu.make_async_copy(query, qin, in_sem.at[0]),
        pltpu.make_async_copy(value_t, wt.at[0], in_sem.at[1]),
        pltpu.make_async_copy(key_t, wt.at[1], in_sem.at[2]),
        pltpu.make_async_copy(gain, gbuf, in_sem.at[3]),
    ]
    big = [pltpu.make_async_copy(ctx.at[v], xbuf.at[v], x_sem.at[v]) for v in (0, 4, 1, 5, 2, 6, 3, 7)]
    for copy in small + big:
        copy.start()
    own_w = pltpu.make_async_copy(out_w, wr.at[head], w_own)
    own_w.start()
    barrier = pltpu.get_barrier_semaphore()
    for k in reversed(OFFSETS[1:]):
        pl.semaphore_signal(barrier, inc=1, device_id={"tok": at(k), "head": head}, device_id_type=MESH)
    for i in range(1, 8):
        pl.semaphore_signal(barrier, inc=1, device_id={"tok": tok, "head": (head + i) % 8}, device_id_type=MESH)

    for copy in small:
        copy.wait()
    row = qin[...].astype(jnp.float32) * HD**-0.5
    row = jnp.concatenate([row, row], axis=1)
    qs[0] = row
    qr[0] = row
    for i in range(GROUP * len(RANKS)):
        if i not in SLOTS:
            qr[i] = jnp.zeros_like(row)

    key_value = jnp.concatenate([wt[1], wt[0]], axis=0)
    value_key = jnp.concatenate([wt[0], wt[1]], axis=0)
    low = lax.broadcasted_iota(jnp.int32, (xbuf.shape[1], 2 * HD), 1) < HD

    def project(v, weights):
        pltpu.make_async_copy(ctx.at[v], xbuf.at[v], x_sem.at[v]).wait()
        data = xbuf[v].astype(jnp.float32)
        meansq = jnp.mean(data * data, axis=-1, keepdims=True)
        normed[v] = (data * lax.rsqrt(meansq + 1e-06) * gbuf[...]).astype(jnp.bfloat16)
        return lax.dot_general(
            normed[v], weights, (((1,), (1,)), ((), ())), preferred_element_type=jnp.float32
        )

    def project_pairs(pairs):
        for i in pairs:
            first, second = project(i, key_value), project(i + HALF, value_key)
            keys_t[i] = jnp.where(low, first, second).astype(jnp.bfloat16).T
            values[i] = jnp.where(low, second, first).astype(jnp.bfloat16)

    project_pairs(range(EARLY))
    pl.semaphore_wait(barrier, N - 1 + 7)
    for j in [j for pair in zip(reversed(range(32, N)), range(1, 32)) for j in pair] + [32]:
        pltpu.make_async_remote_copy(
            src_ref=qs.at[0], dst_ref=qr.at[SLOTS[j]], send_sem=q_send, recv_sem=q_recv.at[SLOTS[j] // GROUP],
            device_id={"tok": at(OFFSETS[j]), "head": head}, device_id_type=MESH,
        ).start()
    for i in range(1, 8):
        pltpu.make_async_remote_copy(
            src_ref=out_w, dst_ref=wr.at[head], send_sem=w_send, recv_sem=w_recv,
            device_id={"tok": tok, "head": (head + i) % 8}, device_id_type=MESH,
        ).start()
    project_pairs(range(EARLY, HALF))

    lane = lax.broadcasted_iota(jnp.int32, (GROUP, 2 * HD), 1)
    all_keys_t = keys_t[...].reshape(HALF * 2 * HD, xbuf.shape[1])
    all_values = jnp.concatenate([values[i] for i in range(HALF)], axis=1)

    def score(d):
        rows = pl.ds(d * GROUP, GROUP)
        both = qr[rows].reshape(GROUP, 2 * HD)
        left, right = jnp.where(lane < HD, both, 0.0), jnp.where(lane < HD, 0.0, both)
        none = jnp.zeros_like(both)
        spread = jnp.concatenate(
            [
                jnp.concatenate(
                    [(left if v < HALF else right) if v % HALF == i else none for v in range(videos)], axis=0
                )
                for i in range(HALF)
            ],
            axis=1,
        ).astype(jnp.bfloat16)
        scores = jnp.dot(spread, all_keys_t, preferred_element_type=jnp.float32)
        top = jnp.max(scores, axis=-1, keepdims=True)
        expo = jnp.exp(scores - top)
        total = jnp.sum(expo, axis=-1, keepdims=True)
        acc = jnp.dot(expo.astype(jnp.bfloat16), all_values, preferred_element_type=jnp.float32)
        stats = jnp.zeros((GROUP, 2 * HD), jnp.float32)
        for v in range(videos):
            own = slice(v * GROUP, (v + 1) * GROUP)
            stats = jnp.where(lane == v, top[own], jnp.where(lane == videos + v, total[own], stats))
        for i in range(HALF):
            lanes = slice(2 * HD * i, 2 * HD * (i + 1))
            low_rows = slice((i + HALF) * GROUP, (i + HALF + 1) * GROUP)
            high_rows = slice(i * GROUP, (i + 1) * GROUP)
            ps[rows, i, :] = jnp.where(lane < HD, acc[low_rows, lanes], acc[high_rows, lanes])
        ps[rows, HALF, :] = stats

    score(0)
    for d, rank in enumerate(RANKS):
        if d > 0:
            came = qr.at[pl.ds(d * GROUP, len(rank))]
            pltpu.make_async_copy(came, came, q_recv.at[d]).wait()
            score(d)
        for k in rank:
            j = OFFSETS.index(k)
            if k == OPPOSITE:
                pr[j] = ps[SLOTS[j]]
            else:
                pltpu.make_async_remote_copy(
                    src_ref=ps.at[SLOTS[j]], dst_ref=pr.at[j], send_sem=p_send, recv_sem=p_recv,
                    device_id={"tok": at(opposite(k)), "head": head}, device_id_type=MESH,
                ).start()

    own_w.wait()
    pltpu.make_async_copy(wr.at[pl.ds(0, 7)], wr.at[pl.ds(0, 7)], w_recv).wait()
    zeros = jnp.zeros((HD, HD), jnp.bfloat16)
    for h in range(8):
        wide = jnp.concatenate([zeros, wr[h]], axis=1)
        wd[pl.ds(2 * HD * h, HD)] = wide
        wide = jnp.concatenate([wr[h], zeros], axis=1)
        wd[pl.ds(2 * HD * h + HD, HD)] = wide

    came = pr.at[pl.ds(0, N - 1)]
    pltpu.make_async_copy(came, came, p_recv).wait()
    stats = pr[:, HALF, :]
    low = lax.broadcasted_iota(jnp.int32, (1, 2 * HD), 1) < HD
    factor = jnp.exp(stats - jnp.max(stats, axis=0, keepdims=True))
    total = jnp.sum(factor * pltpu.roll(stats, 2 * HD - videos, 1), axis=0, keepdims=True)
    attended = []
    for i in range(HALF):
        weight = jnp.where(low, factor[:, i + HALF : i + HALF + 1], factor[:, i : i + 1])
        accum = jnp.sum(weight * pr[:, i, :], axis=0, keepdims=True)
        attended.append(accum / jnp.where(low, total[:, i + HALF : i + HALF + 1], total[:, i : i + 1]))
    att[...] = jnp.concatenate(attended, axis=0).astype(att.dtype)

    mine = ((yh + 1) % 2) * 4 + (x + 2) % 4
    slot = (z + 4) % 8
    for j in reversed(range(1, N)):
        pltpu.make_async_remote_copy(
            src_ref=att, dst_ref=ar.at[head, slot], send_sem=a_send, recv_sem=a_recv,
            device_id={"tok": at(OFFSETS[j]), "head": mine}, device_id_type=MESH,
        ).start()

    @pl.when(mine != head)
    def _():
        pltpu.make_async_remote_copy(
            src_ref=att, dst_ref=ar.at[head, slot], send_sem=a_send, recv_sem=a_recv,
            device_id={"tok": tok, "head": mine}, device_id_type=MESH,
        ).start()

    @pl.when(mine == head)
    def _():
        pltpu.make_async_copy(att, ar.at[head, slot], a_recv).start()

    pltpu.make_async_copy(wr.at[pl.ds(0, 7)], wr.at[pl.ds(0, 7)], w_send).wait()
    gone = qr.at[pl.ds(0, N - 1)]
    pltpu.make_async_copy(gone, gone, q_send).wait()
    gone = ps.at[pl.ds(0, N - 1)]
    pltpu.make_async_copy(gone, gone, p_send).wait()

    pltpu.make_async_copy(ar, ar, a_recv).wait()
    blocks = [ar[h].astype(jnp.float32).reshape(8 * HALF, 2 * HD).astype(jnp.bfloat16) for h in range(8)]
    result = jnp.dot(jnp.concatenate(blocks, axis=1), wd[...], preferred_element_type=jnp.float32)
    result = result.reshape(8, HALF, 2 * HD)
    out[...] = jnp.concatenate([result[:, :, :HD], result[:, :, HD:]], axis=1).astype(out.dtype)

    gone = ar.at[0, pl.ds(0, 7)]
    for _ in range(9):
        pltpu.make_async_copy(gone, gone, a_send).wait()

    @pl.when(mine != head)
    def _():
        pltpu.make_async_copy(att, att, a_send).wait()


def per_device(context, ctx_gain, queries, key_weight, value_weight, out_weight):
    videos, tokens, width = context.shape
    f32, bf16 = jnp.float32, jnp.bfloat16
    anywhere = pl.BlockSpec(memory_space=pl.ANY)
    dma = pltpu.SemaphoreType.DMA
    return pl.pallas_call(
        kernel,
        out_shape=pltpu.VMEM((8, videos, out_weight.shape[1]), bf16),
        in_specs=[anywhere] * 6,
        out_specs=pl.BlockSpec(memory_space=pltpu.VMEM),
        scratch_shapes=[
            pltpu.VMEM((videos, tokens, width), bf16),
            pltpu.VMEM((1, width), f32),
            pltpu.VMEM((1, HD), bf16),
            pltpu.VMEM((2, HD, width), bf16),
            pltpu.VMEM((videos, tokens, width), bf16),
            pltpu.VMEM((HALF, 2 * HD, tokens), bf16),
            pltpu.VMEM((HALF, tokens, 2 * HD), bf16),
            pltpu.VMEM((1, 1, 2 * HD), f32),
            pltpu.VMEM((GROUP * len(RANKS), 1, 2 * HD), f32),
            pltpu.VMEM((GROUP * len(RANKS), HALF + 1, 2 * HD), f32),
            pltpu.VMEM((N, HALF + 1, 2 * HD), f32),
            pltpu.VMEM((HALF, 2 * HD), bf16),
            pltpu.VMEM((8, 8, HALF, 2 * HD), bf16),
            pltpu.VMEM((8, HD, out_weight.shape[1]), bf16),
            pltpu.VMEM((8 * 2 * HD, 2 * HD), bf16),
            dma((4,)), dma((videos,)),
            dma, dma((len(RANKS),)), dma, dma, dma, dma, dma, dma, dma,
        ],
        compiler_params=pltpu.CompilerParams(
            collective_id=0, has_side_effects=True, vmem_limit_bytes=60 * 2**20
        ),
        name="resampler",
    )(context, ctx_gain.reshape(1, width), queries, key_weight.T, value_weight.T, out_weight)


def solution(mesh):
    in_specs = (
        P(None, "tok", None),
        P(),
        P("tok", "head"),
        P(None, "head"),
        P(None, "head"),
        P("head", "tok"),
    )
    out_specs = P("head", None, "tok")
    return jax.shard_map(per_device, mesh=mesh, in_specs=in_specs, out_specs=out_specs, check_vma=False)
```

```python
import functools

import jax
import jax.numpy as jnp
from jax import lax
from jax.experimental import pallas as pl
from jax.experimental.pallas import tpu as pltpu
from jax.sharding import PartitionSpec as P

MESH = pl.DeviceIdType.MESH
HD = 64
GROUP = 8
EARLY = 2
HALF = 4
RING = (2, 4, 8)
HOPS = (4, 1, 1)
OPPOSITE = (1, 2, 4)


def distance(k):
    return sum(min(a, n - a) * w for a, n, w in zip(k, RING, HOPS))


def opposite(k):
    return tuple((o - a) % n for o, a, n in zip(OPPOSITE, k, RING))


EVERY = [(a, b, c) for a in range(2) for b in range(4) for c in range(8)]
RANKS = [[k for k in EVERY if distance(k) == d] for d in range(11)]
OFFSETS = [k for rank in RANKS for k in rank]
RANKS = [OFFSETS[:1]] + [OFFSETS[i : i + GROUP] for i in range(1, len(OFFSETS), GROUP)]
SLOTS = [GROUP * d + i for d, rank in enumerate(RANKS) for i in range(len(rank))]
N = len(OFFSETS)


def kernel(
    ctx, gain, query, key_t, value_t, out_w, out,
    xbuf, gbuf, qin, wt, normed, keys_t, values, qs, qr, ps, pr, att, ar, wr, wd,
    in_sem, x_sem, q_send, q_recv, p_send, p_recv, a_send, a_recv, w_send, w_recv, w_own,
):
    tok, head = lax.axis_index("tok"), lax.axis_index("head")
    yh, x, z = tok // 32, (tok // 8) % 4, tok % 8
    ys = [((yh + a) % 2) * 32 for a in range(2)]
    way = 1 - 2 * (head % 2)
    xs = [((x + 4 + way * a) % 4) * 8 for a in range(4)]
    zs = [(z + 8 + way * a) % 8 for a in range(8)]

    def at(k):
        return ys[k[0]] + xs[k[1]] + zs[k[2]]

    videos = ctx.shape[0]
    small = [
        pltpu.make_async_copy(query, qin, in_sem.at[0]),
        pltpu.make_async_copy(value_t, wt.at[0], in_sem.at[1]),
        pltpu.make_async_copy(key_t, wt.at[1], in_sem.at[2]),
        pltpu.make_async_copy(gain, gbuf, in_sem.at[3]),
    ]
    big = [pltpu.make_async_copy(ctx.at[v], xbuf.at[v], x_sem.at[v]) for v in (0, 4, 1, 5, 2, 6, 3, 7)]
    for copy in small + big:
        copy.start()
    own_w = pltpu.make_async_copy(out_w, wr.at[head], w_own)
    own_w.start()
    barrier = pltpu.get_barrier_semaphore()
    for k in reversed(OFFSETS[1:]):
        pl.semaphore_signal(barrier, inc=1, device_id={"tok": at(k), "head": head}, device_id_type=MESH)
    for i in range(1, 8):
        pl.semaphore_signal(barrier, inc=1, device_id={"tok": tok, "head": (head + i) % 8}, device_id_type=MESH)

    for copy in small:
        copy.wait()
    row = qin[...].astype(jnp.float32) * HD**-0.5
    row = jnp.concatenate([row, row], axis=1)
    qs[0] = row
    qr[0] = row
    for i in range(GROUP * len(RANKS)):
        if i not in SLOTS:
            qr[i] = jnp.zeros_like(row)

    key_value = jnp.concatenate([wt[1], wt[0]], axis=0)
    value_key = jnp.concatenate([wt[0], wt[1]], axis=0)
    low = lax.broadcasted_iota(jnp.int32, (xbuf.shape[1], 2 * HD), 1) < HD

    def project(v, weights):
        pltpu.make_async_copy(ctx.at[v], xbuf.at[v], x_sem.at[v]).wait()
        data = xbuf[v].astype(jnp.float32)
        meansq = jnp.mean(data * data, axis=-1, keepdims=True)
        normed[v] = (data * lax.rsqrt(meansq + 1e-06) * gbuf[...]).astype(jnp.bfloat16)
        return lax.dot_general(
            normed[v], weights, (((1,), (1,)), ((), ())), preferred_element_type=jnp.float32
        )

    def project_pairs(pairs):
        for i in pairs:
            first, second = project(i, key_value), project(i + HALF, value_key)
            keys_t[i] = jnp.where(low, first, second).astype(jnp.bfloat16).T
            values[i] = jnp.where(low, second, first).astype(jnp.bfloat16)

    project_pairs(range(EARLY))
    pl.semaphore_wait(barrier, N - 1 + 7)
    for j in [j for pair in zip(reversed(range(32, N)), range(1, 32)) for j in pair] + [32]:
        pltpu.make_async_remote_copy(
            src_ref=qs.at[0], dst_ref=qr.at[SLOTS[j]], send_sem=q_send, recv_sem=q_recv.at[SLOTS[j] // GROUP],
            device_id={"tok": at(OFFSETS[j]), "head": head}, device_id_type=MESH,
        ).start()
    for i in range(1, 8):
        pltpu.make_async_remote_copy(
            src_ref=out_w, dst_ref=wr.at[head], send_sem=w_send, recv_sem=w_recv,
            device_id={"tok": tok, "head": (head + i) % 8}, device_id_type=MESH,
        ).start()
    project_pairs(range(EARLY, HALF))

    lane = lax.broadcasted_iota(jnp.int32, (GROUP, 2 * HD), 1)
    all_keys_t = keys_t[...].reshape(HALF * 2 * HD, xbuf.shape[1])
    all_values = jnp.concatenate([values[i] for i in range(HALF)], axis=1)

    def score(d):
        rows = pl.ds(d * GROUP, GROUP)
        both = qr[rows].reshape(GROUP, 2 * HD)
        left, right = jnp.where(lane < HD, both, 0.0), jnp.where(lane < HD, 0.0, both)
        none = jnp.zeros_like(both)
        spread = jnp.concatenate(
            [
                jnp.concatenate(
                    [(left if v < HALF else right) if v % HALF == i else none for v in range(videos)], axis=0
                )
                for i in range(HALF)
            ],
            axis=1,
        ).astype(jnp.bfloat16)
        scores = jnp.dot(spread, all_keys_t, preferred_element_type=jnp.float32)
        top = jnp.max(scores, axis=-1, keepdims=True)
        expo = jnp.exp(scores - top)
        total = jnp.sum(expo, axis=-1, keepdims=True)
        acc = jnp.dot(expo.astype(jnp.bfloat16), all_values, preferred_element_type=jnp.float32)
        stats = jnp.zeros((GROUP, 2 * HD), jnp.float32)
        for v in range(videos):
            own = slice(v * GROUP, (v + 1) * GROUP)
            stats = jnp.where(lane == v, top[own], jnp.where(lane == videos + v, total[own], stats))
        for i in range(HALF):
            lanes = slice(2 * HD * i, 2 * HD * (i + 1))
            low_rows = slice((i + HALF) * GROUP, (i + HALF + 1) * GROUP)
            high_rows = slice(i * GROUP, (i + 1) * GROUP)
            ps[rows, i, :] = jnp.where(lane < HD, acc[low_rows, lanes], acc[high_rows, lanes])
        ps[rows, HALF, :] = stats

    score(0)
    for d, rank in enumerate(RANKS):
        if d > 0:
            came = qr.at[pl.ds(d * GROUP, len(rank))]
            pltpu.make_async_copy(came, came, q_recv.at[d]).wait()
            score(d)
        for k in rank:
            j = OFFSETS.index(k)
            if k == OPPOSITE:
                pr[j] = ps[SLOTS[j]]
            else:
                pltpu.make_async_remote_copy(
                    src_ref=ps.at[SLOTS[j]], dst_ref=pr.at[j], send_sem=p_send, recv_sem=p_recv,
                    device_id={"tok": at(opposite(k)), "head": head}, device_id_type=MESH,
                ).start()

    own_w.wait()
    pltpu.make_async_copy(wr.at[pl.ds(0, 7)], wr.at[pl.ds(0, 7)], w_recv).wait()
    zeros = jnp.zeros((HD, HD), jnp.bfloat16)
    for h in range(8):
        wide = jnp.concatenate([zeros, wr[h]], axis=1)
        wd[pl.ds(2 * HD * h, HD)] = wide
        wide = jnp.concatenate([wr[h], zeros], axis=1)
        wd[pl.ds(2 * HD * h + HD, HD)] = wide

    came = pr.at[pl.ds(0, N - 1)]
    pltpu.make_async_copy(came, came, p_recv).wait()
    stats = pr[:, HALF, :]
    low = lax.broadcasted_iota(jnp.int32, (1, 2 * HD), 1) < HD
    factor = jnp.exp(stats - jnp.max(stats, axis=0, keepdims=True))
    total = jnp.sum(factor * pltpu.roll(stats, 2 * HD - videos, 1), axis=0, keepdims=True)
    attended = []
    for i in range(HALF):
        weight = jnp.where(low, factor[:, i + HALF : i + HALF + 1], factor[:, i : i + 1])
        accum = jnp.sum(weight * pr[:, i, :], axis=0, keepdims=True)
        attended.append(accum / jnp.where(low, total[:, i + HALF : i + HALF + 1], total[:, i : i + 1]))
    att[...] = jnp.concatenate(attended, axis=0).astype(att.dtype)

    mine = ((yh + 1) % 2) * 4 + (x + 2) % 4
    slot = (z + 4) % 8
    for j in reversed(range(1, N)):
        pltpu.make_async_remote_copy(
            src_ref=att, dst_ref=ar.at[head, slot], send_sem=a_send, recv_sem=a_recv,
            device_id={"tok": at(OFFSETS[j]), "head": mine}, device_id_type=MESH,
        ).start()

    @pl.when(mine != head)
    def _():
        pltpu.make_async_remote_copy(
            src_ref=att, dst_ref=ar.at[head, slot], send_sem=a_send, recv_sem=a_recv,
            device_id={"tok": tok, "head": mine}, device_id_type=MESH,
        ).start()

    @pl.when(mine == head)
    def _():
        pltpu.make_async_copy(att, ar.at[head, slot], a_recv).start()

    pltpu.make_async_copy(wr.at[pl.ds(0, 7)], wr.at[pl.ds(0, 7)], w_send).wait()
    gone = qr.at[pl.ds(0, N - 1)]
    pltpu.make_async_copy(gone, gone, q_send).wait()
    gone = ps.at[pl.ds(0, N - 1)]
    pltpu.make_async_copy(gone, gone, p_send).wait()

    pltpu.make_async_copy(ar, ar, a_recv).wait()
    blocks = [ar[h].astype(jnp.float32).reshape(8 * HALF, 2 * HD).astype(jnp.bfloat16) for h in range(8)]
    result = jnp.dot(jnp.concatenate(blocks, axis=1), wd[...], preferred_element_type=jnp.float32)
    result = result.reshape(8, HALF, 2 * HD)
    out[...] = jnp.concatenate([result[:, :, :HD], result[:, :, HD:]], axis=1).astype(out.dtype)

    gone = ar.at[0, pl.ds(0, 7)]
    for _ in range(9):
        pltpu.make_async_copy(gone, gone, a_send).wait()

    @pl.when(mine != head)
    def _():
        pltpu.make_async_copy(att, att, a_send).wait()


def per_device(context, ctx_gain, queries, key_weight, value_weight, out_weight):
    videos, tokens, width = context.shape
    f32, bf16 = jnp.float32, jnp.bfloat16
    anywhere = pl.BlockSpec(memory_space=pl.ANY)
    dma = pltpu.SemaphoreType.DMA
    return pl.pallas_call(
        kernel,
        out_shape=pltpu.VMEM((8, videos, out_weight.shape[1]), bf16),
        in_specs=[anywhere] * 6,
        out_specs=pl.BlockSpec(memory_space=pltpu.VMEM),
        scratch_shapes=[
            pltpu.VMEM((videos, tokens, width), bf16),
            pltpu.VMEM((1, width), f32),
            pltpu.VMEM((1, HD), bf16),
            pltpu.VMEM((2, HD, width), bf16),
            pltpu.VMEM((videos, tokens, width), bf16),
            pltpu.VMEM((HALF, 2 * HD, tokens), bf16),
            pltpu.VMEM((HALF, tokens, 2 * HD), bf16),
            pltpu.VMEM((1, 1, 2 * HD), f32),
            pltpu.VMEM((GROUP * len(RANKS), 1, 2 * HD), f32),
            pltpu.VMEM((GROUP * len(RANKS), HALF + 1, 2 * HD), f32),
            pltpu.VMEM((N, HALF + 1, 2 * HD), f32),
            pltpu.VMEM((HALF, 2 * HD), bf16),
            pltpu.VMEM((8, 8, HALF, 2 * HD), bf16),
            pltpu.VMEM((8, HD, out_weight.shape[1]), bf16),
            pltpu.VMEM((8 * 2 * HD, 2 * HD), bf16),
            dma((4,)), dma((videos,)),
            dma, dma((len(RANKS),)), dma, dma, dma, dma, dma, dma, dma,
        ],
        compiler_params=pltpu.CompilerParams(
            collective_id=0, has_side_effects=True, vmem_limit_bytes=60 * 2**20
        ),
        name="resampler",
    )(context, ctx_gain.reshape(1, width), queries, key_weight.T, value_weight.T, out_weight)


def solution(mesh):
    in_specs = (
        P(None, "tok", None),
        P(),
        P("tok", "head"),
        P(None, "head"),
        P(None, "head"),
        P("head", "tok"),
    )
    out_specs = P("head", None, "tok")
    return jax.shard_map(per_device, mesh=mesh, in_specs=in_specs, out_specs=out_specs, check_vma=False)
```
